512 devices in a mesh: section: 8 (over z_lo, core), mp: 64 (over x, z_hi, y).
Axes of the slice: x: 4, y: 4, z: 16 (z_hi: 4, z_lo: 4; z = z_hi * 4 + z_lo), core: 2. Of those that a mesh axis runs over, the one named last changes fastest.
Arguments:
- pending_vectors: bfloat16 [8, 128, 3584], P('section', None, 'mp'), may hold values from -6 to 6
- arriving_learner_vectors: bfloat16 [1, 128, 3584], P(None, None, 'mp'), may hold values from -6 to 6
- mentor_state_vectors: bfloat16 [64, 2, 128, 8192], P('section', None, None, 'mp'), may hold values from -6 to 6
- breadth_mapping_matrix: bfloat16 [8192, 3584], P('mp', 'section'), may hold values from -0.0625 to 0.0625
- rms_gain_factor: float32 [8, 3584], P('section'), may hold values from 0.25 to 1.75
- gating_matrix: bfloat16 [8, 3584, 9472], P('section', None, 'mp'), may hold values from -0.09375 to 0.09375
- lowering_matrix: bfloat16 [8, 9472, 3584], P('section', 'mp'), may hold values from -0.0625 to 0.0625
- mentor_depth_table: int32 [8], replicated, may hold values from 0 to 63, as said below
Outputs:
- grad_gate: bfloat16 [8, 3584, 9472], P('section', None, 'mp')
- grad_down: bfloat16 [8, 9472, 3584], P('section', 'mp')
- distill_loss: float32 [], replicated
The draws below stay inside these ranges and needn't reach their ends.
Inputs may be any that keep to these rules, and one draw needn't show every extreme that they name: `mentor_depth_table`: the entries are distinct teacher depths.
All inputs are finite; a program needn't handle non-finite values.
Results may differ from the reference program's by a relative error of at most 0.011.
Values may be sent and summed in bfloat16 or wider, within the bound.
A program may use at most 64 MiB of HBM per device.

```python
import jax
import jax.numpy as jnp
from jax import lax

LEARNER_BREADTH = 3584
DT = 8192
FF = 9472
MICRO_ITEMS = 128
TICKS = 2
HANDOVER_PARTS = 8
TEACHER_DEPTHS = 64


def draw_mentor_depth_table(key, part):
    key = jax.random.fold_in(key, 11)
    first_key, second_key = jax.random.split(key)
    others = jax.random.permutation(first_key, TEACHER_DEPTHS - 1)[:HANDOVER_PARTS - 1].astype(jnp.int32)
    deepest = jnp.full((1,), TEACHER_DEPTHS - 1, jnp.int32)
    table = jnp.concatenate([others, deepest]).astype(jnp.int32)
    return jax.random.permutation(second_key, table).astype(jnp.int32)


def shard_levels(rng, dims, cuts, low, top_value):
    def one(dim, shards_of):
        steps = jax.random.uniform(jax.random.fold_in(jax.random.fold_in(rng, 6), dim), (shards_of,), jnp.float32, low / len(cuts), top_value / len(cuts))
        return jnp.repeat(jnp.exp(steps), dims[dim] // shards_of).reshape((-1,) + (1,) * (len(dims) - dim - 1))

    level = one(*cuts[0])
    for cut in cuts[1:]:
        level = level * one(*cut)
    return level


def bell_draw(rng, shape, width, bound, cuts=(), dtype=jnp.bfloat16):
    loudness = shard_levels(rng, shape, cuts, -0.22, 0.18) if cuts else 1.0
    array = jax.random.normal(rng, shape, jnp.float32) * width * loudness
    return jnp.minimum(jnp.maximum(array, -bound), bound).astype(dtype)


def setup_inputs(seed: int = 0) -> dict:
    key_of = jax.random.split(jax.random.key(seed), 9)
    pending_vectors = bell_draw(key_of[0], (HANDOVER_PARTS, MICRO_ITEMS, LEARNER_BREADTH), 1.0, 6.0, ((0, 8), (2, 64)))
    arriving_learner_vectors = bell_draw(key_of[1], (TICKS - 1, MICRO_ITEMS, LEARNER_BREADTH), 1.0, 6.0, ((2, 64),))
    mentor_state_vectors = bell_draw(key_of[2], (TEACHER_DEPTHS, TICKS, MICRO_ITEMS, DT), 1.0, 6.0, ((0, 8), (3, 64)))
    breadth_mapping_matrix = bell_draw(key_of[3], (DT, LEARNER_BREADTH), DT ** -0.5, 0.0625, ((0, 64), (1, 8)))
    rms_gain_factor = jnp.clip(1.0 + 0.15 * jax.random.normal(key_of[4], (HANDOVER_PARTS, LEARNER_BREADTH), jnp.float32), 0.25, 1.75)
    gating_matrix = bell_draw(key_of[5], (HANDOVER_PARTS, LEARNER_BREADTH, FF), LEARNER_BREADTH ** -0.5, 0.09375, ((0, 8), (2, 64)))
    lowering_matrix = bell_draw(key_of[6], (HANDOVER_PARTS, FF, LEARNER_BREADTH), FF ** -0.5, 0.0625, ((0, 8), (1, 64)))
    mentor_depth_table = draw_mentor_depth_table(jax.random.fold_in(key_of[8], 71), 0)
    return dict(pending_vectors=pending_vectors, arriving_learner_vectors=arriving_learner_vectors, mentor_state_vectors=mentor_state_vectors, breadth_mapping_matrix=breadth_mapping_matrix, rms_gain_factor=rms_gain_factor, gating_matrix=gating_matrix, lowering_matrix=lowering_matrix, mentor_depth_table=mentor_depth_table)


def normalize(held, gain):
    values = held.astype(jnp.float32)
    spread = lax.optimization_barrier(jnp.mean(values * values, axis=-1, keepdims=True))
    return (values * jax.lax.rsqrt(spread + 1e-06) * gain).astype(jnp.bfloat16)

def reference(pending_vectors, arriving_learner_vectors, mentor_state_vectors, breadth_mapping_matrix, rms_gain_factor, gating_matrix, lowering_matrix, mentor_depth_table):
    targets = []
    for part_index in range(HANDOVER_PARTS):
        chosen = mentor_state_vectors[mentor_depth_table[part_index]].reshape(TICKS * MICRO_ITEMS, DT)
        mapped = jnp.dot(chosen, breadth_mapping_matrix, preferred_element_type=jnp.float32).astype(jnp.bfloat16)
        targets.append(mapped.reshape(TICKS, MICRO_ITEMS, LEARNER_BREADTH))
    kept_vectors = [pending_vectors[part_index] for part_index in range(HANDOVER_PARTS)]
    gate_acc = [jnp.zeros((LEARNER_BREADTH, FF), jnp.float32) for part_index in range(HANDOVER_PARTS)]
    down_acc = [jnp.zeros((FF, LEARNER_BREADTH), jnp.float32) for part_index in range(HANDOVER_PARTS)]
    objective = jnp.zeros((), jnp.float32)
    for moment in range(TICKS):
        outputs = []
        for part_index in range(HANDOVER_PARTS):
            held = kept_vectors[part_index]
            normed = normalize(held, rms_gain_factor[part_index])
            gate_sum = jnp.dot(normed, gating_matrix[part_index], preferred_element_type=jnp.float32)
            activated = jax.nn.silu(gate_sum).astype(jnp.bfloat16)
            mixed = jnp.dot(activated, lowering_matrix[part_index], preferred_element_type=jnp.float32)
            output = (held.astype(jnp.float32) + mixed).astype(jnp.bfloat16)
            outputs.append(output)
            differ = output.astype(jnp.float32) - targets[part_index][moment].astype(jnp.float32)
            objective = objective + jnp.sum(differ * differ) / (2.0 * MICRO_ITEMS)
            delta = (differ / MICRO_ITEMS).astype(jnp.bfloat16)
            down_acc[part_index] = down_acc[part_index] + jnp.dot(activated.T, delta, preferred_element_type=jnp.float32)
            back = jnp.dot(delta, lowering_matrix[part_index].T, preferred_element_type=jnp.float32)
            sigma = jax.nn.sigmoid(gate_sum)
            slope = (back * sigma * (1.0 + gate_sum * (1.0 - sigma))).astype(jnp.bfloat16)
            gate_acc[part_index] = gate_acc[part_index] + jnp.dot(normed.T, slope, preferred_element_type=jnp.float32)
        if moment + 1 < TICKS:
            kept_vectors = [arriving_learner_vectors[moment]] + outputs[:-1]
    grad_gate = jnp.stack(gate_acc).astype(jnp.bfloat16)
    grad_down = jnp.stack(down_acc).astype(jnp.bfloat16)
    distill_loss = objective / (HANDOVER_PARTS * TICKS * LEARNER_BREADTH)
    return (grad_gate, grad_down, distill_loss)
```

```python
import functools

import jax
import jax.numpy as jnp
from jax import lax
from jax.experimental import pallas as pl
from jax.experimental.pallas import tpu as pltpu
from jax.sharding import PartitionSpec as P

F32 = jnp.float32
BF16 = jnp.bfloat16
MESH = pl.DeviceIdType.MESH

X, Z, Y = 4, 4, 4
ZL, CORES = 4, 2


def round_up(value, step):
    return (value + step - 1) // step * step


def kernel(
    dims,
    table,
    pend,
    arriving,
    teacher,
    mapping,
    gain,
    gate,
    low,
    grad_gate,
    grad_down,
    loss,
    gz,
    full,
    part,
    tpart,
    r1,
    t1,
    s1,
    u1,
    r2,
    t2,
    zs,
    tz,
    r3,
    t3,
    share,
    nat,
    gain_cols,
    low_nat,
    low_rows,
    map_all,
    map_nat,
    map_rows,
    sel_out,
    sel_own,
    sel_in,
    sel_far,
    normed,
    delta,
    act,
    gsum,
    slope,
    lz,
    lx,
    ly,
    ll,
    lc,
    send_sem,
    recv_sem,
):
    width, rows, tokens, ff = dims
    pad = round_up(rows, 16)
    half = Z // 2
    long = half * rows
    sections = ZL * CORES
    sec, mp = lax.axis_index("section"), lax.axis_index("mp")
    x, z, y = mp // (Z * Y), mp // Y % Z, mp % Y
    zl, core = sec // CORES, sec % CORES

    def at_x(d):
        return (sec, lax.rem(x + d, X) * (Z * Y) + z * Y + y)

    def at_z(d):
        return (sec, x * (Z * Y) + lax.rem(z + d, Z) * Y + y)

    def at_y(d):
        return (sec, x * (Z * Y) + z * Y + lax.rem(y + d, Y))

    def at_zl(d):
        return (lax.rem(zl + d, ZL) * CORES + core, mp)

    sibling = (zl * CORES + 1 - core, mp)
    following = (lax.rem(sec + 1, sections), mp)
    previous = (lax.rem(sec + sections - 1, sections), mp)

    firsts = (at_y, at_x)
    seconds = (at_x, at_y)
    coords = ((y, x), (x, y))

    used = [0]
    unsent = []

    def send(src, dst, device):
        k = used[0]
        used[0] += 1
        copy = pltpu.make_async_remote_copy(
            src_ref=src,
            dst_ref=dst,
            send_sem=send_sem.at[k],
            recv_sem=recv_sem.at[k],
            device_id=device,
            device_id_type=MESH,
        )
        copy.start()
        unsent.append(copy)
        return copy

    def arrived(copies):
        for copy in copies:
            copy.wait_recv()

    def flush():
        for copy in unsent:
            copy.wait_send()
        unsent.clear()

    def natural(h, i1, i2, k):
        bx, by = (i2, i1) if h == 0 else (i1, i2)
        return pl.multiple_of(((bx * Z + h * half + k) * Y + by) * rows, 8)

    def padded(values):
        if pad == rows:
            return values
        return jnp.concatenate([values, jnp.zeros((pad - rows, tokens), F32)], axis=0)

    def gather_z(a):
        return [send(gz.at[a, z], gz.at[a, z], at_z(d)) for d in range(1, Z)]

    def gather_first(a, copies):
        arrived(copies)
        near, far = [], []
        for h in range(2):
            block = jnp.concatenate(
                [gz[a, h * half + k].astype(F32)[:rows] for k in range(half)], axis=0
            )
            c1, c2 = coords[h]
            full[a, h, c1, c2] = block.astype(BF16)
        for h in range(2):
            c1, c2 = coords[h]
            ref = full.at[a, h, c1, c2]
            near.append([send(ref, ref, seconds[h](d)) for d in range(1, X)])
        for h in range(2):
            c1, c2 = coords[h]
            ref = full.at[a, h, c1, c2]
            far.extend(send(ref, ref, firsts[h](d)) for d in range(1, X))
        return near, far

    def gather_second(a, state):
        near, far = state
        for e in range(1, X):
            for h in range(2):
                near[h][e - 1].wait_recv()
                c1, c2 = coords[h]
                ref = full.at[a, h, c1, lax.rem(c2 + X - e, X)]
                far.extend(send(ref, ref, firsts[h](d)) for d in range(1, X))
        return far

    def reduce_first(src, dst):
        copies = [[], []]
        for d in range(1, X):
            for h in range(2):
                c1, _ = coords[h]
                copies[h].append(
                    send(src.at[h, lax.rem(c1 + d, X)], dst.at[h, d - 1], firsts[h](d))
                )
        return copies

    def reduce_second(src, got, sums, dst, copies):
        out = [[], []]
        for h in range(2):
            arrived(copies[h])
            c1, c2 = coords[h]
            for i in range(X):
                total = src[h, c1, i].astype(F32)
                for d in range(X - 1):
                    total = total + got[h, d, i].astype(F32)
                sums[h, i] = total.astype(BF16)
            for d in range(1, X):
                out[h].append(send(sums.at[h, lax.rem(c2 + d, X)], dst.at[h, d - 1], seconds[h](d)))
        return out

    def reduce_third(sums, got, dst, landing, copies, count):
        for h in range(2):
            arrived(copies[h])
            _, c2 = coords[h]
            total = sums[h, c2].astype(F32)
            for d in range(X - 1):
                total = total + got[h, d].astype(F32)
            for j in range(count):
                for k in range(half):
                    start = j * long + k * rows
                    piece = padded(total[start : start + rows])
                    dst[h * half + k, j * pad : (j + 1) * pad] = piece.astype(BF16)
        return [
            send(dst.at[lax.rem(z + d, Z)], landing.at[d - 1], at_z(d)) for d in range(1, Z)
        ]

    def reduce_end(src, got, copies):
        arrived(copies)
        total = src[z].astype(F32)
        for d in range(Z - 1):
            total = total + got[d].astype(F32)
        return total

    peers = [at_x(d) for d in range(1, X)] + [at_z(d) for d in range(1, Z)]
    peers += [at_y(d) for d in range(1, Y)] + [at_zl(d) for d in range(1, ZL)]
    peers += [sibling, following, previous]
    barrier = pltpu.get_barrier_semaphore()
    for peer in peers:
        pl.semaphore_signal(barrier, inc=1, device_id=peer, device_id_type=MESH)
    held_first = padded(pend[...].astype(F32))
    gz[0, z] = held_first.astype(BF16)
    map_all[sec] = mapping[...]
    zeros = jnp.zeros((2 * tokens, teacher.shape[2]), BF16)

    def chosen_for(to):
        local = teacher.shape[0]
        depth = table[to] - sec * local
        mine = jnp.logical_and(depth >= 0, depth < local)
        block = teacher[jnp.clip(depth, 0, local - 1)]
        return jnp.where(mine, block, zeros)

    for i in range(ZL):
        sel_out[i] = chosen_for(i * CORES + 1 - core)
        sel_own[i] = chosen_for(i * CORES + core)
    pl.semaphore_wait(barrier, len(peers))

    gathered = gather_z(0)
    sel_copy = send(sel_out, sel_in, sibling)
    map_copies = [send(map_all.at[sec], map_all.at[sec], at_zl(d)) for d in range(1, ZL)]
    map_other = [send(map_all.at[sec], map_all.at[sec], sibling)]

    state = gather_first(0, gathered)

    for c in range(width // 128):
        line = jnp.broadcast_to(gain[:, c * 128 : (c + 1) * 128], (128, 128))
        gain_cols[c * 128 : (c + 1) * 128, :] = line.T
        low_nat[c * 128 : (c + 1) * 128, :] = low[:, c * 128 : (c + 1) * 128].astype(F32).T

    far = gather_second(0, state)

    sel_copy.wait_recv()
    for i in range(ZL):
        sel_own[i] = sel_own[i] + sel_in[i]
    sel_copies = [
        send(sel_own.at[lax.rem(zl + d, ZL)], sel_far.at[d - 1], at_zl(d)) for d in range(1, ZL)
    ]

    def order_rows(src, dst):
        for h in range(2):
            for i1 in range(X):
                for i2 in range(X):
                    block = jnp.concatenate(
                        [src[pl.ds(natural(h, i1, i2, k), rows), :] for k in range(half)], axis=0
                    )
                    start = ((h * X + i1) * X + i2) * long
                    dst[start : start + long, :] = block.astype(BF16)

    order_rows(low_nat, low_rows)

    for e in range(1, ZL):
        map_copies[e - 1].wait_recv()
        ref = map_all.at[lax.rem(zl + ZL - e, ZL) * CORES + core]
        map_other.append(send(ref, ref, sibling))

    def assemble(a):
        square = jnp.zeros((8, tokens), F32)
        for h in range(2):
            for i1 in range(X):
                for i2 in range(X):
                    block = full[a, h, i1, i2].astype(F32)
                    square = square + jnp.sum((block * block).reshape(-1, 8, tokens), axis=0)
                    for k in range(half):
                        start = natural(h, i1, i2, k)
                        nat[pl.ds(start, rows), :] = block[k * rows : (k + 1) * rows]
        return square

    def forward(t, a):
        square = assemble(a)
        spread = jnp.sum(square, axis=0, keepdims=True) / width
        factor = lax.rsqrt(spread + 1e-06)
        lanes = slice(t * tokens, (t + 1) * tokens)
        step = 128
        for c in range(width // step):
            block = slice(c * step, (c + 1) * step)
            normed[block, lanes] = (nat[block, :] * factor * gain_cols[block, :]).astype(BF16)
        gate_sum = jnp.dot(gate[...], normed[:, lanes], preferred_element_type=F32)
        gsum[t] = gate_sum
        activated = (gate_sum * (1.0 / (1.0 + jnp.exp(-gate_sum)))).astype(BF16)
        act[:, lanes] = activated
        size = X * X * long
        for h in range(2):
            for i1 in range(X):
                start = (h * X + i1) * X * long
                got = jnp.dot(
                    low_rows[start : start + X * long, :], activated, preferred_element_type=F32
                )
                part[t, h, i1] = got.astype(BF16).reshape(X, long, tokens)

    arrived(far)
    forward(0, 0)
    reduced = reduce_first(part.at[0], r1.at[0])

    arrived(sel_copies)
    chosen = sel_own[zl]
    for d in range(ZL - 1):
        chosen = chosen + sel_far[d]
    arrived(map_other)
    for s in range(sections):
        rows_of = map_all.shape[1]
        map_nat[s * rows_of : (s + 1) * rows_of, :] = map_all[s].astype(F32)
    order_rows(map_nat, map_rows)
    for h in range(2):
        for i1 in range(X):
            start = (h * X + i1) * X * long
            for t in range(2):
                got = lax.dot_general(
                    map_rows[start : start + X * long, :],
                    chosen[t * tokens : (t + 1) * tokens],
                    (((1,), (1,)), ((), ())),
                    preferred_element_type=F32,
                )
                tpart[h, i1, :, t * long : (t + 1) * long, :] = got.astype(BF16).reshape(
                    X, long, tokens
                )
    treduced = reduce_first(tpart, t1)

    reduced = reduce_second(part.at[0], r1.at[0], s1.at[0], r2.at[0], reduced)
    reduced = reduce_third(s1.at[0], r2.at[0], zs.at[0], r3.at[0], reduced, 1)
    mixed = reduce_end(zs.at[0], r3.at[0], reduced)
    output0 = (held_first.astype(F32) + mixed).astype(BF16)
    share[0] = output0
    passed = send(share.at[0], share.at[1], following)
    passed.wait_recv()
    entering = padded(arriving[...].astype(F32))
    held_second = jnp.where(sec == 0, entering, share[1].astype(F32))
    gz[1, z] = held_second.astype(BF16)
    gathered = gather_z(1)

    treduced = reduce_second(tpart, t1, u1, t2, treduced)
    state = gather_first(1, gathered)
    far = gather_second(1, state)
    treduced = reduce_third(u1, t2, tz, t3, treduced, 2)
    flush()
    arrived(far)
    forward(1, 1)
    reduced = reduce_first(part.at[1], r1.at[1])

    def differ_of(output, target):
        return output.astype(F32) - target.astype(F32)

    target = reduce_end(tz, t3, treduced).astype(BF16)
    differ0 = differ_of(share[0], target[:pad])
    gz[2, z] = (differ0 / tokens).astype(BF16)
    gathered0 = gather_z(2)
    reduced = reduce_second(part.at[1], r1.at[1], s1.at[1], r2.at[1], reduced)
    state0 = gather_first(2, gathered0)
    reduced = reduce_third(s1.at[1], r2.at[1], zs.at[1], r3.at[1], reduced, 1)
    far0 = gather_second(2, state0)
    mixed = reduce_end(zs.at[1], r3.at[1], reduced)
    output1 = (held_second + mixed).astype(BF16)
    differ1 = differ_of(output1, target[pad:])
    gz[3, z] = (differ1 / tokens).astype(BF16)
    gathered1 = gather_z(3)

    square = differ0 * differ0 + differ1 * differ1
    square = jnp.sum(square.reshape(-1, 8, tokens), axis=0)

    def exchange(buffer, mine, values, sends):
        buffer[mine] = values
        return [send(buffer.at[mine], buffer.at[mine], device) for device in sends]

    def summed(buffer, copies):
        arrived(copies)
        total = buffer[0]
        for i in range(1, buffer.shape[0]):
            total = total + buffer[i]
        return total

    loss_copies = exchange(lz, z, square, [at_z(d) for d in range(1, Z)])

    def assemble_delta(t, a):
        lanes = slice(t * tokens, (t + 1) * tokens)
        assemble(a)
        step = 128
        for c in range(width // step):
            block = slice(c * step, (c + 1) * step)
            delta[block, lanes] = nat[block, :].astype(BF16)

    def backward(t):
        lanes = slice(t * tokens, (t + 1) * tokens)
        back = jnp.dot(low[...], delta[:, lanes], preferred_element_type=F32)
        gate_sum = gsum[t]
        sigma = 1.0 / (1.0 + jnp.exp(-gate_sum))
        slope[:, lanes] = (back * sigma * (1.0 + gate_sum * (1.0 - sigma))).astype(BF16)

    state1 = gather_first(3, gathered1)
    square = summed(lz, loss_copies)
    loss_copies = exchange(lx, x, square, [at_x(d) for d in range(1, X)])
    far1 = gather_second(3, state1)
    square = summed(lx, loss_copies)
    loss_copies = exchange(ly, y, square, [at_y(d) for d in range(1, Y)])
    arrived(far0)
    assemble_delta(0, 2)
    backward(0)
    square = summed(ly, loss_copies)
    loss_copies = exchange(ll, zl, square, [at_zl(d) for d in range(1, ZL)])
    flush()
    square = summed(ll, loss_copies)
    loss_copies = exchange(lc, core, square, [sibling])
    arrived(far1)
    assemble_delta(1, 3)
    backward(1)
    turned = (((1,), (1,)), ((), ()))
    step = 512 if width % 512 == 0 else 128
    for c in range(width // step):
        block = slice(c * step, (c + 1) * step)
        got = lax.dot_general(slope[...], normed[block, :], turned, preferred_element_type=F32)
        grad_gate[:, block] = got.astype(BF16)
        got = lax.dot_general(act[...], delta[block, :], turned, preferred_element_type=F32)
        grad_down[:, block] = got.astype(BF16)
    square = summed(lc, loss_copies)
    objective = jnp.sum(square) / (2.0 * tokens)
    loss[0, 0] = objective / (sections * 2 * width)
    flush()


def copies_needed():
    gather = (Z - 1) + 2 * (X - 1) + 2 * (X - 1) + 2 * (X - 1) * (X - 1)
    reduce = 4 * (X - 1) + (Z - 1)
    section = 1 + (ZL - 1) + (ZL - 1) + ZL + 1
    loss = (Z - 1) + (X - 1) + (Y - 1) + (ZL - 1) + 1
    return 4 * gather + 3 * reduce + section + loss


def local(
    pending_vectors,
    arriving_learner_vectors,
    mentor_state_vectors,
    breadth_mapping_matrix,
    rms_gain_factor,
    gating_matrix,
    lowering_matrix,
    mentor_depth_table,
):
    width = gating_matrix.shape[1]
    ff = gating_matrix.shape[2]
    tokens, rows = pending_vectors.shape[1:]
    depths, feats = mentor_state_vectors.shape[0], mentor_state_vectors.shape[3]
    pad = round_up(rows, 16)
    long = Z // 2 * rows
    columns = breadth_mapping_matrix.shape[1]
    vmem = pl.BlockSpec(memory_space=pltpu.VMEM)
    smem = pl.BlockSpec(memory_space=pltpu.SMEM)
    copies = copies_needed()
    scratch = [
        pltpu.VMEM((4, Z, pad, tokens), BF16),
        pltpu.VMEM((4, 2, X, X, long, tokens), BF16),
        pltpu.VMEM((2, 2, X, X, long, tokens), BF16),
        pltpu.VMEM((2, X, X, 2 * long, tokens), BF16),
        pltpu.VMEM((2, 2, X - 1, X, long, tokens), BF16),
        pltpu.VMEM((2, X - 1, X, 2 * long, tokens), BF16),
        pltpu.VMEM((2, 2, X, long, tokens), BF16),
        pltpu.VMEM((2, X, 2 * long, tokens), BF16),
        pltpu.VMEM((2, 2, X - 1, long, tokens), BF16),
        pltpu.VMEM((2, X - 1, 2 * long, tokens), BF16),
        pltpu.VMEM((2, Z, pad, tokens), BF16),
        pltpu.VMEM((Z, 2 * pad, tokens), BF16),
        pltpu.VMEM((2, Z - 1, pad, tokens), BF16),
        pltpu.VMEM((Z - 1, 2 * pad, tokens), BF16),
        pltpu.VMEM((2, pad, tokens), BF16),
        pltpu.VMEM((width, tokens), F32),
        pltpu.VMEM((width, tokens), F32),
        pltpu.VMEM((width, ff), F32),
        pltpu.VMEM((width, ff), BF16),
        pltpu.VMEM((ZL * CORES, columns, feats), BF16),
        pltpu.VMEM((width, feats), F32),
        pltpu.VMEM((width, feats), BF16),
        pltpu.VMEM((ZL, 2 * tokens, feats), BF16),
        pltpu.VMEM((ZL, 2 * tokens, feats), BF16),
        pltpu.VMEM((ZL, 2 * tokens, feats), BF16),
        pltpu.VMEM((ZL - 1, 2 * tokens, feats), BF16),
        pltpu.VMEM((width, 2 * tokens), BF16),
        pltpu.VMEM((width, 2 * tokens), BF16),
        pltpu.VMEM((ff, 2 * tokens), BF16),
        pltpu.VMEM((2, ff, tokens), F32),
        pltpu.VMEM((ff, 2 * tokens), BF16),
        pltpu.VMEM((Z, 8, tokens), F32),
        pltpu.VMEM((X, 8, tokens), F32),
        pltpu.VMEM((Y, 8, tokens), F32),
        pltpu.VMEM((ZL, 8, tokens), F32),
        pltpu.VMEM((CORES, 8, tokens), F32),
        pltpu.SemaphoreType.DMA((copies,)),
        pltpu.SemaphoreType.DMA((copies,)),
    ]
    grad_gate, grad_down, loss = pl.pallas_call(
        functools.partial(kernel, (width, rows, tokens, ff)),
        out_shape=(
            jax.ShapeDtypeStruct((ff, width), BF16),
            jax.ShapeDtypeStruct((ff, width), BF16),
            jax.ShapeDtypeStruct((1, 1), F32),
        ),
        in_specs=[smem] + [vmem] * 7,
        out_specs=(vmem, vmem, smem),
        scratch_shapes=scratch,
        compiler_params=pltpu.CompilerParams(
            collective_id=0, has_side_effects=True, vmem_limit_bytes=56 * 1024 * 1024
        ),
    )(
        mentor_depth_table,
        pending_vectors[0].T,
        arriving_learner_vectors[0].T,
        mentor_state_vectors.reshape(depths, 2 * tokens, feats),
        breadth_mapping_matrix.T,
        rms_gain_factor,
        gating_matrix[0].T,
        lowering_matrix[0],
    )
    return grad_gate.T[None], grad_down[None], loss[0, 0]


def solution(mesh):
    in_specs = (
        P("section", None, "mp"),
        P(None, None, "mp"),
        P("section", None, None, "mp"),
        P("mp", "section"),
        P("section", None),
        P("section", None, "mp"),
        P("section", "mp", None),
        P(),
    )
    out_specs = (P("section", None, "mp"), P("section", "mp", None), P())
    return jax.shard_map(local, mesh=mesh, in_specs=in_specs, out_specs=out_specs, check_vma=False)
```

```python
import functools

import jax
import jax.numpy as jnp
from jax import lax
from jax.experimental import pallas as pl
from jax.experimental.pallas import tpu as pltpu
from jax.sharding import PartitionSpec as P

F32 = jnp.float32
BF16 = jnp.bfloat16
MESH = pl.DeviceIdType.MESH

X, Z, Y = 4, 4, 4
ZL, CORES = 4, 2


def round_up(value, step):
    return (value + step - 1) // step * step


def kernel(
    dims,
    table,
    pend,
    arriving,
    teacher,
    mapping,
    gain,
    gate,
    low,
    grad_gate,
    grad_down,
    loss,
    gz,
    came,
    full,
    part,
    tpart,
    r1,
    t1,
    s1,
    u1,
    r2,
    t2,
    zs,
    tz,
    share,
    nat,
    gain_cols,
    low_nat,
    low_rows,
    map_all,
    map_rows,
    sel_out,
    sel_own,
    sel_in,
    sel_far,
    normed,
    delta,
    act,
    gsum,
    slope,
    lx,
    ly,
    lc,
    send_sem,
    recv_sem,
):
    width, rows, tokens, ff = dims
    pad = round_up(rows, 16)
    half = Z // 2
    long = half * rows
    sections = ZL * CORES
    sec, mp = lax.axis_index("section"), lax.axis_index("mp")
    x, z, y = mp // (Z * Y), mp // Y % Z, mp % Y
    zl, core = sec // CORES, sec % CORES

    def at_x(d):
        return (sec, lax.rem(x + d, X) * (Z * Y) + z * Y + y)

    def at_z(d):
        return (sec, x * (Z * Y) + lax.rem(z + d, Z) * Y + y)

    def at_y(d):
        return (sec, x * (Z * Y) + z * Y + lax.rem(y + d, Y))

    def at_zl(d):
        return (lax.rem(zl + d, ZL) * CORES + core, mp)

    sibling = (zl * CORES + 1 - core, mp)

    firsts = (at_y, at_x)
    seconds = (at_x, at_y)
    coords = ((y, x), (x, y))
    away = range(1, X)

    def at_section(d):
        return (lax.rem(sec + d, sections), mp)

    def at_next(peer):
        return (lax.rem(sec + 1, sections), peer[1])

    def at_previous(peer):
        return (lax.rem(sec + sections - 1, sections), peer[1])

    used = [0]
    unsent = []

    def send(src, dst, device):
        k = used[0]
        used[0] += 1
        copy = pltpu.make_async_remote_copy(
            src_ref=src,
            dst_ref=dst,
            send_sem=send_sem.at[k],
            recv_sem=recv_sem.at[k],
            device_id=device,
            device_id_type=MESH,
        )
        copy.start()
        unsent.append(copy)
        return copy

    def arrived(copies):
        for copy in copies:
            copy.wait_recv()

    def flush():
        for copy in unsent:
            copy.wait_send()
        unsent.clear()

    def natural(h, i1, i2, k):
        bx, by = (i2, i1) if h == 0 else (i1, i2)
        return pl.multiple_of(((bx * Z + h * half + k) * Y + by) * rows, 8)

    def padded(values):
        if pad == rows:
            return values
        return jnp.concatenate([values, jnp.zeros((pad - rows, tokens), F32)], axis=0)

    def line_start(b):
        return [send(gz.at[b, z], gz.at[b, z], at_z(d)) for d in range(1, Z)]

    def line_block(b, h):
        block = [gz[b, h * half + k].astype(F32)[:rows] for k in range(half)]
        return jnp.concatenate(block, axis=0).astype(BF16)

    def nothing():
        pass

    def gather_first(a):
        near, far = [[], []], []
        for d in away:
            for h in range(2):
                c1, c2 = coords[h]
                ref = full.at[a, h, c1, c2]
                near[h].append(send(ref, ref, seconds[h](d)))
        spread_out(a, 0, far)
        return near, far

    def spread_out(a, e, far):
        for d in range(1, X):
            for h in range(2):
                c1, c2 = coords[h]
                i2 = lax.rem(c2 + X - e, X)
                ref = full.at[a, h, c1, i2]
                far.append((send(ref, ref, firsts[h](d)), h, lax.rem(c1 + X - d, X), i2))

    def gather_second(a, state, also=nothing):
        near, far = state
        also()
        for e in range(1, X):
            for h in range(2):
                near[h][e - 1].wait_recv()
            spread_out(a, e, far)
        return far

    def gather_end(a, far):
        square = jnp.zeros((8, tokens), F32)

        def place(h, i1, i2, square):
            block = full[a, h, i1, i2].astype(F32)
            for k in range(half):
                nat[pl.ds(natural(h, i1, i2, k), rows), :] = block[k * rows : (k + 1) * rows]
            return square + jnp.sum((block * block).reshape(-1, 8, tokens), axis=0)

        for h in range(2):
            c1, c2 = coords[h]
            for e in range(X):
                square = place(h, c1, lax.rem(c2 + X - e, X), square)
        for copy, h, i1, i2 in far:
            copy.wait_recv()
            square = place(h, i1, i2, square)
        return square

    first_part, last_part = pl.ds(1, X // 2), pl.ds(X // 2 + 1, X // 2 - 1)

    def reduce_first(compute, src, dst):
        early, late, own = [[], []], [[], []], [[], []]
        for d in range(1, X):
            for h in range(2):
                compute(h, d)
                for refs, span in ((early, first_part), (late, last_part)):
                    if span.size:
                        refs[h].append(
                            send(src.at[h, d, span], dst.at[h, d - 1, span], firsts[h](d))
                        )
        for d in range(1, X):
            for h in range(2):
                own[h].append(send(src.at[h, d, 0], dst.at[h, d - 1, 0], firsts[h](d)))
        for h in range(2):
            compute(h, 0)
        return early, late, own

    def reduce_second(src, got, sums, dst, copies):
        out = [[], []]
        spans = (
            range(1, X // 2 + 1),
            range(X // 2 + 1, X),
            range(1),
        )
        for span, group in zip(spans, copies):
            for h in range(2):
                arrived(group[h])
                for i in span:
                    total = src[h, 0, i].astype(F32)
                    for d in range(X - 1):
                        total = total + got[h, d, i].astype(F32)
                    sums[h, i] = total.astype(BF16)
                    if i:
                        out[h].append(send(sums.at[h, i], dst.at[h, i - 1], seconds[h](i)))
        return out

    def reduce_third(sums, got, lines, copies):
        out = []
        for h in range(2):
            arrived(copies[h])
            total = sums[h, 0].astype(F32)
            for d in range(X - 1):
                total = total + got[h, d].astype(F32)
            lines[z, h] = total.astype(BF16)
            ref = lines.at[z, h]
            out.extend(send(ref, ref, at_z(d)) for d in (2, 1, 3))
        return out

    def reduce_end(lines, copies):
        arrived(copies)
        total = lines[0].astype(F32)
        for i in range(1, Z):
            total = total + lines[i].astype(F32)
        return total

    beside = [at_x(d) for d in away] + [at_y(d) for d in away]
    peers = beside + [at_z(d) for d in range(1, Z)]
    peers += [at_section(d) for d in range(1, sections)]
    peers += [at_next(peer) for peer in beside] + [at_previous(peer) for peer in beside]
    barrier = pltpu.get_barrier_semaphore()
    for peer in peers:
        pl.semaphore_signal(barrier, inc=1, device_id=peer, device_id_type=MESH)
    gz[0, z] = padded(pend[...].astype(F32)).astype(BF16)
    gz[1, z] = padded(arriving[...].astype(F32)).astype(BF16)
    pl.semaphore_wait(barrier, len(peers))
    line0 = line_start(0)

    map_all[sec] = mapping[...]
    zeros = jnp.zeros((2 * tokens, teacher.shape[2]), BF16)

    def chosen_for(to):
        local = teacher.shape[0]
        depth = table[to] - sec * local
        mine = jnp.logical_and(depth >= 0, depth < local)
        block = teacher[jnp.clip(depth, 0, local - 1)]
        return jnp.where(mine, block, zeros)

    for i in range(ZL):
        sel_out[i] = chosen_for(i * CORES + 1 - core)
        sel_own[i] = chosen_for(i * CORES + core)
    sel_copy = send(sel_out, sel_in, sibling)
    for c in range(width // 128):
        low_nat[c * 128 : (c + 1) * 128, :] = low[:, c * 128 : (c + 1) * 128].astype(F32).T

    for c in range(width // 128):
        line = jnp.broadcast_to(gain[:, c * 128 : (c + 1) * 128], (128, 128))
        gain_cols[c * 128 : (c + 1) * 128, :] = line.T
    sel_copy.wait_recv()
    for i in range(ZL):
        sel_own[i] = sel_own[i] + sel_in[i]

    arrived(line0)
    for h in range(2):
        c1, c2 = coords[h]
        full[0, h, c1, c2] = line_block(0, h)
    state = gather_first(0)
    sel_copies = [
        send(sel_own.at[lax.rem(zl + d, ZL)], sel_far.at[d - 1], at_zl(d)) for d in range(1, ZL)
    ]
    map_copies = [send(map_all.at[sec], map_all.at[sec], at_zl(d)) for d in range(1, ZL)]
    map_other = [send(map_all.at[sec], map_all.at[sec], sibling)]
    line1 = line_start(1)
    far = gather_second(0, state)

    for h in range(2):
        c1, c2 = coords[h]
        for d1 in range(X):
            for d2 in range(X):
                i1, i2 = lax.rem(c1 + d1, X), lax.rem(c2 + d2, X)
                block = jnp.concatenate(
                    [low_nat[pl.ds(natural(h, i1, i2, k), rows), :] for k in range(half)], axis=0
                )
                low_rows[h, d1, d2 * long : (d2 + 1) * long, :] = block.astype(BF16)

    def forward(t, square):
        spread = jnp.sum(square, axis=0, keepdims=True) / width
        factor = lax.rsqrt(spread + 1e-06)
        lanes = slice(t * tokens, (t + 1) * tokens)
        step = 128
        for c in range(width // step):
            block = slice(c * step, (c + 1) * step)
            normed[block, lanes] = (nat[block, :] * factor * gain_cols[block, :]).astype(BF16)
        gate_sum = jnp.dot(gate[...], normed[:, lanes], preferred_element_type=F32)
        gsum[t] = gate_sum
        activated = (gate_sum * (1.0 / (1.0 + jnp.exp(-gate_sum)))).astype(BF16)
        act[:, lanes] = activated

        def lowered(h, d):
            got = jnp.dot(low_rows[h, d], activated, preferred_element_type=F32)
            part[t, h, d] = got.astype(BF16).reshape(X, long, tokens)

        return reduce_first(lowered, part.at[t], r1.at[t])

    reduced = forward(0, gather_end(0, far))
    reduced = reduce_second(part.at[0], r1.at[0], s1.at[0], r2.at[0], reduced)
    for e in range(1, ZL):
        map_copies[e - 1].wait_recv()
        ref = map_all.at[lax.rem(zl + ZL - e, ZL) * CORES + core]
        map_other.append(send(ref, ref, sibling))
    reduced = reduce_third(s1.at[0], r2.at[0], zs.at[0], reduced)

    arrived(line1)
    came_copies = []
    for h in range(2):
        _, c2 = coords[h]
        came[0, h, c2] = line_block(1, h)
        ref = came.at[0, h, c2]
        came_copies.extend(send(ref, ref, seconds[h](d)) for d in away)

    arrived(sel_copies)
    chosen = sel_own[zl]
    for d in range(ZL - 1):
        chosen = chosen + sel_far[d]
    arrived(map_other)
    for s in range(sections):
        i, h = s // CORES, s % CORES
        block = map_all[s].astype(F32)
        c1, c2 = coords[h]
        for j in range(Y):
            piece = jnp.concatenate(
                [block[(k * Y + j) * rows : (k * Y + j + 1) * rows] for k in range(half)], axis=0
            )
            i1, i2 = (j, i) if h == 0 else (i, j)
            d1, d2 = lax.rem(i1 + X - c1, X), lax.rem(i2 + X - c2, X)
            map_rows[h, d1, d2] = piece.astype(BF16)

    def targets(h, d):
        for t in range(2):
            got = lax.dot_general(
                map_rows[h, d].reshape(X * long, -1),
                chosen[t * tokens : (t + 1) * tokens],
                (((1,), (1,)), ((), ())),
                preferred_element_type=F32,
            )
            tpart[h, d, :, t * long : (t + 1) * long, :] = got.astype(BF16).reshape(
                X, long, tokens
            )

    treduced = reduce_first(targets, tpart, t1)

    def share_of(a):
        return jnp.stack([full[a, h, coords[h][0], coords[h][1]] for h in range(2)]).astype(F32)

    mixed = reduce_end(zs.at[0], reduced)
    share[...] = (share_of(0) + mixed).astype(BF16)
    passed = {}
    for d in range(X):
        for h in range(2):
            c2 = coords[h][1]
            peer = seconds[h](d) if d else (sec, mp)
            passed[h, d] = send(share.at[h], came.at[1, h, c2], at_next(peer))
    arrived(came_copies)
    far = []
    for e in range(X):
        for h in range(2):
            c1, c2 = coords[h]
            i2 = lax.rem(c2 + X - e, X)
            passed[h, e].wait_recv()
            full[1, h, c1, i2] = jnp.where(sec == 0, came[0, h, i2], came[1, h, i2])
        spread_out(1, e, far)
    treduced = reduce_second(tpart, t1, u1, t2, treduced)
    flush()
    treduced = reduce_third(u1, t2, tz, treduced)
    reduced = forward(1, gather_end(1, far))

    def differ_of(output, target):
        return output.astype(F32) - target.astype(F32)

    def start_delta(a, differ):
        for h in range(2):
            full[a, h, coords[h][0], coords[h][1]] = (differ[h] / tokens).astype(BF16)
        return gather_first(a)

    reduced = reduce_second(part.at[1], r1.at[1], s1.at[1], r2.at[1], reduced)
    reduced = reduce_third(s1.at[1], r2.at[1], zs.at[1], reduced)
    target = reduce_end(tz, treduced).astype(BF16)
    differ0 = differ_of(share[...], target[:, :long])
    state0 = start_delta(2, differ0)
    far0 = gather_second(2, state0)
    mixed = reduce_end(zs.at[1], reduced)
    output1 = (share_of(1) + mixed).astype(BF16)
    differ1 = differ_of(output1, target[:, long:])
    square = differ0 * differ0 + differ1 * differ1
    square = jnp.sum(square.reshape(-1, 8, tokens), axis=0)

    def exchange(buffer, mine, values, sends):
        buffer[mine] = values
        return [send(buffer.at[mine], buffer.at[mine], device) for device in sends]

    def summed(buffer, copies):
        arrived(copies)
        total = buffer[0]
        for i in range(1, buffer.shape[0]):
            total = total + buffer[i]
        return total

    loss_copies = [exchange(lx, x, square, [at_x(d) for d in away])]
    state1 = start_delta(3, differ1)

    def loss_y():
        values = summed(lx, loss_copies[0])
        loss_copies[0] = exchange(ly, y, values, [at_y(d) for d in away])

    def gather_delta(t, a, far):
        lanes = slice(t * tokens, (t + 1) * tokens)
        gather_end(a, far)
        step = 128
        for c in range(width // step):
            block = slice(c * step, (c + 1) * step)
            delta[block, lanes] = nat[block, :].astype(BF16)

    def backward(t):
        lanes = slice(t * tokens, (t + 1) * tokens)
        back = jnp.dot(low[...], delta[:, lanes], preferred_element_type=F32)
        gate_sum = gsum[t]
        sigma = 1.0 / (1.0 + jnp.exp(-gate_sum))
        slope[:, lanes] = (back * sigma * (1.0 + gate_sum * (1.0 - sigma))).astype(BF16)

    far1 = gather_second(3, state1, loss_y)
    values = summed(ly, loss_copies[0])
    loss_copies[0] = exchange(lc, sec, values, [at_section(d) for d in range(1, sections)])
    gather_delta(0, 2, far0)
    backward(0)
    flush()
    gather_delta(1, 3, far1)
    backward(1)
    turned = (((1,), (1,)), ((), ()))
    step = 512 if width % 512 == 0 else 128
    for c in range(width // step):
        block = slice(c * step, (c + 1) * step)
        got = lax.dot_general(slope[...], normed[block, :], turned, preferred_element_type=F32)
        grad_gate[:, block] = got.astype(BF16)
        got = lax.dot_general(act[...], delta[block, :], turned, preferred_element_type=F32)
        grad_down[:, block] = got.astype(BF16)
    square = summed(lc, loss_copies[0])
    objective = jnp.sum(square) / (2.0 * tokens)
    loss[0, 0] = objective / (sections * 2 * width)
    flush()


def copies_needed():
    line = 2 * (Z - 1)
    gather = 2 * X * (X - 1)
    near = 2 * (X - 1)
    reduce = 8 * (X - 1) + 2 * (Z - 1)
    section = 1 + (ZL - 1) + (ZL - 1) + ZL + 2 * X
    loss = (X - 1) + (Y - 1) + (ZL * CORES - 1)
    return line + 4 * (gather + near) + 3 * reduce + section + loss


def local(
    pending_vectors,
    arriving_learner_vectors,
    mentor_state_vectors,
    breadth_mapping_matrix,
    rms_gain_factor,
    gating_matrix,
    lowering_matrix,
    mentor_depth_table,
):
    width = gating_matrix.shape[1]
    ff = gating_matrix.shape[2]
    tokens, rows = pending_vectors.shape[1:]
    depths, feats = mentor_state_vectors.shape[0], mentor_state_vectors.shape[3]
    pad = round_up(rows, 16)
    long = Z // 2 * rows
    columns = breadth_mapping_matrix.shape[1]
    vmem = pl.BlockSpec(memory_space=pltpu.VMEM)
    smem = pl.BlockSpec(memory_space=pltpu.SMEM)
    copies = copies_needed()
    scratch = [
        pltpu.VMEM((2, Z, pad, tokens), BF16),
        pltpu.VMEM((2, 2, X, long, tokens), BF16),
        pltpu.VMEM((4, 2, X, X, long, tokens), BF16),
        pltpu.VMEM((2, 2, X, X, long, tokens), BF16),
        pltpu.VMEM((2, X, X, 2 * long, tokens), BF16),
        pltpu.VMEM((2, 2, X - 1, X, long, tokens), BF16),
        pltpu.VMEM((2, X - 1, X, 2 * long, tokens), BF16),
        pltpu.VMEM((2, 2, X, long, tokens), BF16),
        pltpu.VMEM((2, X, 2 * long, tokens), BF16),
        pltpu.VMEM((2, 2, X - 1, long, tokens), BF16),
        pltpu.VMEM((2, X - 1, 2 * long, tokens), BF16),
        pltpu.VMEM((2, Z, 2, long, tokens), BF16),
        pltpu.VMEM((Z, 2, 2 * long, tokens), BF16),
        pltpu.VMEM((2, long, tokens), BF16),
        pltpu.VMEM((width, tokens), F32),
        pltpu.VMEM((width, tokens), F32),
        pltpu.VMEM((width, ff), F32),
        pltpu.VMEM((2, X, X * long, ff), BF16),
        pltpu.VMEM((ZL * CORES, columns, feats), BF16),
        pltpu.VMEM((2, X, X, long, feats), BF16),
        pltpu.VMEM((ZL, 2 * tokens, feats), BF16),
        pltpu.VMEM((ZL, 2 * tokens, feats), BF16),
        pltpu.VMEM((ZL, 2 * tokens, feats), BF16),
        pltpu.VMEM((ZL - 1, 2 * tokens, feats), BF16),
        pltpu.VMEM((width, 2 * tokens), BF16),
        pltpu.VMEM((width, 2 * tokens), BF16),
        pltpu.VMEM((ff, 2 * tokens), BF16),
        pltpu.VMEM((2, ff, tokens), F32),
        pltpu.VMEM((ff, 2 * tokens), BF16),
        pltpu.VMEM((X, 8, tokens), F32),
        pltpu.VMEM((Y, 8, tokens), F32),
        pltpu.VMEM((ZL * CORES, 8, tokens), F32),
        pltpu.SemaphoreType.DMA((copies,)),
        pltpu.SemaphoreType.DMA((copies,)),
    ]
    grad_gate, grad_down, loss = pl.pallas_call(
        functools.partial(kernel, (width, rows, tokens, ff)),
        out_shape=(
            jax.ShapeDtypeStruct((ff, width), BF16),
            jax.ShapeDtypeStruct((ff, width), BF16),
            jax.ShapeDtypeStruct((1, 1), F32),
        ),
        in_specs=[smem] + [vmem] * 7,
        out_specs=(vmem, vmem, smem),
        scratch_shapes=scratch,
        compiler_params=pltpu.CompilerParams(
            collective_id=0, has_side_effects=True, vmem_limit_bytes=56 * 1024 * 1024
        ),
    )(
        mentor_depth_table,
        pending_vectors[0].T,
        arriving_learner_vectors[0].T,
        mentor_state_vectors.reshape(depths, 2 * tokens, feats),
        breadth_mapping_matrix.T,
        rms_gain_factor,
        gating_matrix[0].T,
        lowering_matrix[0],
    )
    return grad_gate.T[None], grad_down[None], loss[0, 0]


def solution(mesh):
    in_specs = (
        P("section", None, "mp"),
        P(None, None, "mp"),
        P("section", None, None, "mp"),
        P("mp", "section"),
        P("section", None),
        P("section", None, "mp"),
        P("section", "mp", None),
        P(),
    )
    out_specs = (P("section", None, "mp"), P("section", "mp", None), P())
    return jax.shard_map(local, mesh=mesh, in_specs=in_specs, out_specs=out_specs, check_vma=False)
```
